32 devices in a mesh: pix: 8 (over z, core), date: 4 (over y, x).
Axes of the slice: x: 2, y: 2, z: 4, core: 2. Of those that a mesh axis runs over, the one named last changes fastest.
Arguments:
- pixel_factor: float32 [16384, 256], P(('pix', 'date')), may hold values from -1.5 to 1.5
- date_factor: float32 [3072, 256], P(('date', 'pix')), may hold values from -1.5 to 1.5
- clear_obs: bfloat16 [8, 4, 32, 128, 128], P('pix', 'date'), may hold values from -6 to 6
- clear_blocks: int32 [8, 4, 32], P('pix', 'date'), may hold values from 0 to 95, as said below
- clear_count: int32 [8, 4], P('pix', 'date'), may hold values from 1 to 32, as said below
Outputs:
- pixel_next: float32 [16384, 256], P(('pix', 'date'))
- date_next: float32 [3072, 256], P(('date', 'pix'))
The draws below stay inside these ranges and needn't reach their ends.
Inputs may be any that keep to these rules, and one draw needn't show every extreme that they name: `clear_blocks`: within one tile the 32 entries are distinct block numbers; only the first clear_count entries are clear blocks, later slots carry no observations. `clear_count`: counts are uneven over tiles; at least one tile has exactly 32 clear blocks.
All inputs are finite; a program needn't handle non-finite values.
Results may differ from the reference program's by a relative error of at most 0.013.
Values may be sent and summed in bfloat16 or wider, within the bound.
A program may use at most 64 MiB of HBM per device.

```python
import jax
import jax.numpy as jnp
from jax import lax

BLOCK = 128
R = 256
RB = 16
CB = 6
ITERS = 2
CAP = 32
P_DEV = 2048
C_DEV = 768
PIXELS = 16384
COLS = 3072
N_PIX = 8
N_DATE = 4


def tile_counts(key):
    base = jax.random.fold_in(key, 11)
    tiles = N_PIX * N_DATE
    spread = jax.random.randint(jax.random.fold_in(base, 1), (tiles,), 0, CAP - 1)
    counts = 1 + spread * spread // (CAP - 1)
    forced = jax.random.randint(jax.random.fold_in(base, 3), (), 0, tiles)
    counts = jnp.where(jnp.arange(tiles) == forced, CAP, counts)
    return counts.reshape(N_PIX, N_DATE).astype(jnp.int32)


def draw_clear_count(key, part):
    return tile_counts(key)


def draw_clear_blocks(key, part):
    tiles = N_PIX * N_DATE
    keys = jax.random.split(jax.random.fold_in(key, 29), tiles)
    orders = jax.vmap(lambda single: jax.random.permutation(single, RB * CB))(keys)
    return orders[:, :CAP].reshape(N_PIX, N_DATE, CAP).astype(jnp.int32)


def steps_of(rng, extent, pieces, least, top_value):
    loudness, own = 1.0, jax.random.fold_in(rng, 6)
    for dim, shards_of in pieces:
        draws = jnp.exp(jax.random.uniform(jax.random.fold_in(own, dim), (shards_of,), jnp.float32, least / len(pieces), top_value / len(pieces)))
        loudness = loudness * jnp.repeat(draws, extent[dim] // shards_of).reshape([-1 if axis == dim else 1 for axis in range(len(extent))])
    return loudness


def gaussian(stream_key, shape, deviation, reach, shards=(), kind=jnp.bfloat16):
    drawn = jax.random.normal(stream_key, shape, jnp.float32) * deviation
    if len(shards) > 0:
        drawn = steps_of(stream_key, shape, shards, -0.22, 0.18) * drawn
    return jnp.clip(drawn, min=-reach, max=reach).astype(kind)


def setup_inputs(seed: int = 0) -> dict:
    seeds = jax.random.split(jax.random.key(seed), 6)
    pixel_factor = gaussian(seeds[0], (PIXELS, R), 0.25, 1.5, ((0, 32),), jnp.float32)
    date_factor = gaussian(seeds[1], (COLS, R), 0.25, 1.5, ((0, 32),), jnp.float32)
    clear_obs = gaussian(seeds[2], (N_PIX, N_DATE, CAP, BLOCK, BLOCK), 1.0, 6.0, ((0, 8), (1, 4)))
    clear_blocks = draw_clear_blocks(jax.random.fold_in(seeds[5], 71), 0)
    clear_count = draw_clear_count(jax.random.fold_in(seeds[5], 71), 0)
    return {"pixel_factor": pixel_factor, "date_factor": date_factor, "clear_obs": clear_obs, "clear_blocks": clear_blocks, "clear_count": clear_count}


def block_terms(pixel_panel, date_panel, observed, blocks, filled):
    rank_width = pixel_panel.shape[1]
    row_blocks = pixel_panel.shape[0] // BLOCK
    col_blocks = date_panel.shape[0] // BLOCK
    capacity = blocks.shape[0]
    row_index = (blocks // col_blocks).astype(jnp.int32)
    col_index = (blocks % col_blocks).astype(jnp.int32)
    pixel_tiles = pixel_panel.reshape(row_blocks, BLOCK, rank_width)[row_index].astype(jnp.float32)
    date_tiles = date_panel.reshape(col_blocks, BLOCK, rank_width)[col_index].astype(jnp.float32)
    predicted = jnp.einsum("kir,kjr->kij", pixel_tiles, date_tiles)
    living = (jnp.arange(capacity) < filled)[:, None, None]
    misfit = jnp.where(living, predicted - observed.astype(jnp.float32), 0.0).astype(jnp.bfloat16).astype(jnp.float32)
    pixel_terms = jnp.einsum("kij,kjr->kir", misfit, date_tiles)
    date_terms = jnp.einsum("kij,kir->kjr", misfit, pixel_tiles)
    pixel_grad = jnp.zeros((row_blocks, BLOCK, rank_width), jnp.float32).at[row_index].add(pixel_terms)
    date_grad = jnp.zeros((col_blocks, BLOCK, rank_width), jnp.float32).at[col_index].add(date_terms)
    return pixel_grad.reshape(-1, rank_width), date_grad.reshape(-1, rank_width)


def reference(pixel_factor, date_factor, clear_obs, clear_blocks, clear_count):
    pixel_now = pixel_factor
    date_now = date_factor
    for step in range(ITERS):
        pixel_half = pixel_now.astype(jnp.bfloat16)
        date_half = date_now.astype(jnp.bfloat16)
        date_panels = date_half.reshape(N_DATE, C_DEV, R)

        def band(carry, index):
            panel = lax.dynamic_slice_in_dim(pixel_half, index * P_DEV, P_DEV, 0)

            def tile(unused, dindex):
                pixel_grad, date_grad = block_terms(panel, date_panels[dindex], clear_obs[index, dindex], clear_blocks[index, dindex], clear_count[index, dindex])
                pixel_grad = lax.optimization_barrier(pixel_grad.astype(jnp.bfloat16)).astype(jnp.float32)
                return unused, (pixel_grad, date_grad)

            unused, (pixel_parts, date_parts) = lax.scan(tile, jnp.zeros((), jnp.float32), jnp.arange(N_DATE).astype(jnp.int32))
            return carry + date_parts.reshape(COLS, R), jnp.sum(pixel_parts, axis=0)

        date_grad, pixel_bands = lax.scan(band, jnp.zeros((COLS, R), jnp.float32), jnp.arange(N_PIX).astype(jnp.int32))
        pixel_grad = pixel_bands.reshape(PIXELS, R)
        pixel_now = pixel_now - (64.0 / COLS) * pixel_grad
        date_now = date_now - (64.0 / PIXELS) * date_grad
    return pixel_now, date_now
```

```python
import functools

import jax
import jax.numpy as jnp
from jax import lax
from jax.experimental import pallas as pl
from jax.experimental.pallas import tpu as pltpu
from jax.sharding import PartitionSpec as P

BLOCK = 128
ITERS = 2
MESH = pl.DeviceIdType.MESH
BF = jnp.bfloat16
F32 = jnp.float32


def dot(a, b, ca, cb):
    return lax.dot_general(a, b, (((ca,), (cb,)), ((), ())), preferred_element_type=F32)


def kernel(
    n_pix, n_date, rate_u, rate_v,
    slot_ref, live_ref, u_ref, v_ref, obs_hbm, u_out, v_out,
    obs, ubuf, vbuf, gus, gur, gvs, gvr, vpan, mbuf, gvt, own_gu,
    obs_sem, us, ur, vs, vr, gu_s, gu_r, gv_s, gv_r,
):
    me_p = lax.axis_index("pix")
    me_d = lax.axis_index("date")
    ru, rank = u_ref.shape
    rv = v_ref.shape[0]
    nb = ru // BLOCK
    cols = n_pix * rv
    cb = cols // BLOCK

    load = pltpu.make_async_copy(obs_hbm, obs, obs_sem)
    load.start()

    def at_date(s):
        return lax.rem(me_d + s, n_date)

    def at_pix(s):
        return lax.rem(me_p + s, n_pix)

    def copy(src, dst, ssem, rsem, p, d):
        return pltpu.make_async_remote_copy(
            src_ref=src, dst_ref=dst, send_sem=ssem, recv_sem=rsem, device_id=(p, d), device_id_type=MESH
        )

    def u_copy(t, s):
        return copy(ubuf.at[t, me_d], ubuf.at[t, me_d], us.at[t, s], ur.at[t, s], me_p, at_date(s))

    def v_copy(t, s):
        return copy(vbuf.at[t, me_p], vbuf.at[t, me_p], vs.at[t, s], vr.at[t, s], at_pix(s), me_d)

    def gu_copy(t, s):
        return copy(gus.at[t, s], gur.at[t, s], gu_s.at[t, s], gu_r.at[t, s], me_p, at_date(s))

    def gv_copy(t, s):
        return copy(gvs.at[t, at_pix(s)], gvr.at[t, s], gv_s.at[t, s], gv_r.at[t, s], at_pix(s), me_d)

    barrier = pltpu.get_barrier_semaphore()
    for s in range(1, n_date):
        pl.semaphore_signal(barrier, inc=1, device_id=(me_p, at_date(s)), device_id_type=MESH)
    for s in range(1, n_pix):
        pl.semaphore_signal(barrier, inc=1, device_id=(at_pix(s), me_d), device_id_type=MESH)
    ubuf[0, me_d] = u_ref[...].astype(BF)
    vbuf[0, me_p] = v_ref[...].astype(BF)
    pl.semaphore_wait(barrier, n_date + n_pix - 2)

    def chunk(t, source, store):
        uc = ubuf.at[t, source]

        def rows(ib, carry):
            first = pl.multiple_of(ib * BLOCK, BLOCK)
            predicted = dot(uc[pl.ds(first, BLOCK), :], vpan[...], 1, 1)
            for j in range(cb):
                b = (source * nb + ib) * cb + j
                o = obs[slot_ref[b]].astype(F32)
                m = (predicted[:, j * BLOCK:(j + 1) * BLOCK] - o) * live_ref[b]
                mbuf[pl.ds(first, BLOCK), j * BLOCK:(j + 1) * BLOCK] = m.astype(BF)
            return carry

        lax.fori_loop(0, nb, rows, 0)
        misfit = mbuf[...]
        store(dot(misfit, vpan[...], 1, 0).astype(BF))
        return dot(uc[...], misfit, 0, 0)

    u_prev, v_prev = u_ref, v_ref
    for t in range(ITERS):
        for s in range(1, n_pix):
            v_copy(t, s).start()
        for s in range(1, n_date):
            u_copy(t, s).start()
        if t == 0:
            load.wait()
        for s in range(1, n_pix):
            v_copy(t, s).wait_recv()
        panel = vbuf[t]
        if rv % 16:
            panel = panel.astype(F32)
        vpan[...] = panel.reshape(cols, rank).astype(BF)

        def keep(g):
            own_gu[...] = g

        gvt[...] = chunk(t, me_d, keep)

        def step(s, carry):
            u_copy(t, n_date - s).wait_recv()

            def send(g):
                gus[t, s] = g

            gvt[...] += chunk(t, at_date(s), send)
            gu_copy(t, s).start()
            return carry

        lax.fori_loop(1, n_date, step, 0)
        gv = gvt[...].T.reshape(n_pix, rv, rank)
        gvs[t] = gv.astype(BF)
        for s in range(1, n_pix):
            gv_copy(t, s).start()

        total = gvs[t, me_p].astype(F32)
        for s in range(1, n_pix):
            gv_copy(t, s).wait_recv()
            total += gvr[t, s].astype(F32)
        v_out[...] = v_prev[...] - rate_v * total
        if t + 1 < ITERS:
            vbuf[t + 1, me_p] = v_out[...].astype(BF)
        total = own_gu[...].astype(F32)
        for s in range(1, n_date):
            gu_copy(t, s).wait_recv()
            total += gur[t, s].astype(F32)
        u_out[...] = u_prev[...] - rate_u * total
        if t + 1 < ITERS:
            ubuf[t + 1, me_d] = u_out[...].astype(BF)
        u_prev, v_prev = u_out, v_out

    for t in range(ITERS):
        for s in range(1, n_pix):
            v_copy(t, s).wait_send()
            gv_copy(t, s).wait_send()
        for s in range(1, n_date):
            u_copy(t, s).wait_send()
            gu_copy(t, s).wait_send()


def shards(n_pix, n_date, pixel_factor, date_factor, clear_obs, clear_blocks, clear_count):
    ru, rank = pixel_factor.shape
    rv = date_factor.shape[0]
    devices = n_pix * n_date
    cap = clear_obs.shape[2]
    cols = n_pix * rv
    blocks_in_tile = (n_date * ru // BLOCK) * (cols // BLOCK)
    match = (clear_blocks[0, 0][None, :] == jnp.arange(blocks_in_tile)[:, None]) & (
        jnp.arange(cap)[None, :] < clear_count[0, 0]
    )
    slot = jnp.sum(jnp.where(match, jnp.arange(cap)[None, :], 0), axis=1).astype(jnp.int32)
    live = jnp.sum(match.astype(F32), axis=1)
    body = functools.partial(
        kernel, n_pix, n_date, 64.0 / (rv * devices), 64.0 / (ru * devices)
    )
    vmem = pl.BlockSpec(memory_space=pltpu.VMEM)
    smem = pl.BlockSpec(memory_space=pltpu.SMEM)
    dma = pltpu.SemaphoreType.DMA
    return pl.pallas_call(
        body,
        out_shape=(
            jax.ShapeDtypeStruct((ru, rank), F32),
            jax.ShapeDtypeStruct((rv, rank), F32),
        ),
        in_specs=[smem, smem, vmem, vmem, pl.BlockSpec(memory_space=pl.ANY)],
        out_specs=(vmem, vmem),
        scratch_shapes=[
            pltpu.VMEM((cap, BLOCK, BLOCK), BF),
            pltpu.VMEM((ITERS, n_date, ru, rank), BF),
            pltpu.VMEM((ITERS, n_pix, rv, rank), BF),
            pltpu.VMEM((ITERS, n_date, ru, rank), BF),
            pltpu.VMEM((ITERS, n_date, ru, rank), BF),
            pltpu.VMEM((ITERS, n_pix, rv, rank), BF),
            pltpu.VMEM((ITERS, n_pix, rv, rank), BF),
            pltpu.VMEM((cols, rank), BF),
            pltpu.VMEM((ru, cols), BF),
            pltpu.VMEM((rank, cols), F32),
            pltpu.VMEM((ru, rank), BF),
            dma,
            dma((ITERS, n_date)), dma((ITERS, n_date)),
            dma((ITERS, n_pix)), dma((ITERS, n_pix)),
            dma((ITERS, n_date)), dma((ITERS, n_date)),
            dma((ITERS, n_pix)), dma((ITERS, n_pix)),
        ],
        compiler_params=pltpu.CompilerParams(
            collective_id=0, has_side_effects=True, vmem_limit_bytes=48 * 1024 * 1024
        ),
    )(slot, live, pixel_factor, date_factor, clear_obs.reshape(cap, BLOCK, BLOCK))


def solution(mesh):
    in_specs = (
        P(("pix", "date"), None),
        P(("date", "pix"), None),
        P("pix", "date", None, None, None),
        P("pix", "date", None),
        P("pix", "date"),
    )
    out_specs = (P(("pix", "date"), None), P(("date", "pix"), None))
    body = functools.partial(shards, mesh.shape["pix"], mesh.shape["date"])
    return jax.shard_map(body, mesh=mesh, in_specs=in_specs, out_specs=out_specs, check_vma=False)
```

```python
import functools

import jax
import jax.numpy as jnp
from jax import lax
from jax.experimental import pallas as pl
from jax.experimental.pallas import tpu as pltpu
from jax.sharding import PartitionSpec as P

BLOCK = 128
ITERS = 2
MESH = pl.DeviceIdType.MESH
BF = jnp.bfloat16
F32 = jnp.float32


def dot(a, b, ca, cb):
    return lax.dot_general(a, b, (((ca,), (cb,)), ((), ())), preferred_element_type=F32)


def kernel(
    n_pix, n_date, rate_u, rate_v,
    slot_ref, live_ref, u_hbm, v_hbm, obs_hbm, u_out, v_out,
    u_ref, v_ref, obs, ubuf, vbuf, gus, gur, gvf, gvs, gvr, gve, gvo, vpan, mbuf, gvt, own_gu, keep,
    load_sem, us, ur, vs, vr, ws, wr, gu_s, gu_r, gv_s, gv_r, ge_s, ge_r,
):
    me_p = lax.axis_index("pix")
    me_d = lax.axis_index("date")
    ru, rank = u_ref.shape
    rv = v_ref.shape[0]
    cols = n_pix * rv
    cb = cols // BLOCK
    chips = n_pix // 2
    square = n_date == 4 and ru % (2 * BLOCK) == 0
    half = ru // 2
    piece = mbuf.shape[0]
    nb = piece // BLOCK

    load_u = pltpu.make_async_copy(u_hbm, u_ref, load_sem.at[0])
    load_v = pltpu.make_async_copy(v_hbm, v_ref, load_sem.at[1])
    load_o = pltpu.make_async_copy(obs_hbm, obs, load_sem.at[2])
    load_u.start()
    load_v.start()
    load_o.start()

    core = lax.rem(me_p, 2)
    sib = me_p + 1 - 2 * core

    def at_date(s):
        return lax.rem(me_d + s, n_date)

    def at_chip(k):
        return lax.rem(me_p + 2 * k, n_pix)

    xn = me_d + 1 - 2 * lax.rem(me_d, 2)
    yn = lax.rem(me_d + 2, n_date)
    diag = lax.rem(xn + 2, n_date)

    def copy(src, dst, ssem, rsem, p, d):
        return pltpu.make_async_remote_copy(
            src_ref=src, dst_ref=dst, send_sem=ssem, recv_sem=rsem, device_id=(p, d), device_id_type=MESH
        )

    def v_copy(t, k):
        return copy(vbuf.at[t, me_p], vbuf.at[t, me_p], vs.at[t, k], vr.at[t, k], at_chip(k), me_d)

    def v_pass(t, k):
        held = vbuf.at[t, at_chip(chips - k)]
        return copy(held, held, ws.at[t, k], wr.at[t, k], sib, me_d)

    def ge_copy(t):
        return copy(gve.at[t], gvo.at[t], ge_s.at[t], ge_r.at[t], sib, me_d)

    def gv_copy(t, k):
        return copy(gvs.at[t, k], gvr.at[t, k], gv_s.at[t, k], gv_r.at[t, k], at_chip(k), me_d)

    def u_copy(t, s):
        return copy(ubuf.at[t, me_d], ubuf.at[t, me_d], us.at[t, s], ur.at[t, s], me_p, at_date(s))

    def gu_copy(t, s):
        return copy(gus.at[t, s], gur.at[t, s], gu_s.at[t, s], gu_r.at[t, s], me_p, at_date(s))

    def u_square(t, i):
        owner, h, to = (
            (me_d, 0, xn), (me_d, 1, yn), (me_d, 1, xn), (me_d, 0, yn), (xn, 0, yn), (yn, 1, xn),
        )[i]
        part = ubuf.at[t, owner, pl.ds(h * half, half)]
        return copy(part, part, us.at[t, i], ur.at[t, i], me_p, to)

    def gu_square(t, i):
        to = xn if i in (0, 2, 5) else yn
        return copy(gus.at[t, i], gur.at[t, i], gu_s.at[t, i], gu_r.at[t, i], me_p, to)

    barrier = pltpu.get_barrier_semaphore()

    def greet(p, d):
        pl.semaphore_signal(barrier, inc=1, device_id=(p, d), device_id_type=MESH)

    greet(sib, me_d)
    for k in range(1, chips):
        greet(at_chip(k), me_d)
    if square:
        greet(me_p, xn)
        greet(me_p, yn)
    else:
        for s in range(1, n_date):
            greet(me_p, at_date(s))
    load_u.wait()
    ubuf[0, me_d] = u_ref[...].astype(BF)
    load_v.wait()
    vbuf[0, me_p] = v_ref[...].astype(BF)
    pl.semaphore_wait(barrier, chips + (2 if square else n_date - 1))

    def tile(t, source, start):
        uc = ubuf.at[t, source, pl.ds(start, piece)]
        base = source * (ru // BLOCK) + start // BLOCK

        def rows(ib, carry):
            first = pl.multiple_of(ib * BLOCK, BLOCK)
            predicted = dot(uc[pl.ds(first, BLOCK), :], vpan[...], 1, 1)
            for j in range(cb):
                b = (base + ib) * cb + j
                o = obs[slot_ref[b]].astype(F32)
                m = (predicted[:, j * BLOCK:(j + 1) * BLOCK] - o) * live_ref[b]
                mbuf[pl.ds(first, BLOCK), j * BLOCK:(j + 1) * BLOCK] = m.astype(BF)
            return carry

        lax.fori_loop(0, nb, rows, 0)
        misfit = mbuf[...]
        return dot(misfit, vpan[...], 1, 0), dot(uc[...], misfit, 0, 0)

    def date_start(t):
        for k in range(1, chips):
            v_copy(t, k).start()
        v_pass(t, 0).start()

    def date_pass(t):
        for k in range(1, chips):
            v_copy(t, k).wait_recv()
            v_pass(t, k).start()

    def date_panel(t):
        for k in range(chips):
            v_pass(t, k).wait_recv()
        panel = vbuf[t]
        if rv % 16:
            panel = panel.astype(F32)
        vpan[...] = panel.reshape(cols, rank).astype(BF)

    def pixel_pass(t):
        u_square(t, 0).wait_recv()
        u_square(t, 4).start()
        u_square(t, 1).wait_recv()
        u_square(t, 5).start()

    def date_grad_send(t):
        gvf[...] = gvt[...].T.reshape(n_pix, rv, rank)
        for k in range(chips):
            gve[t, k] = gvf[2 * k + 1 - core].astype(BF)
        ge_copy(t).start()

    def date_grad_pass(t):
        ge_copy(t).wait_recv()
        chip = me_p // 2
        for k in range(1, chips):
            to = lax.rem(chip + k, chips)
            gvs[t, k] = (gvf[2 * to + core] + gvo[t, to].astype(F32)).astype(BF)
            gv_copy(t, k).start()

    def date_update(t, v_prev):
        total = gvf[me_p] + gvo[t, me_p // 2].astype(F32)
        for k in range(1, chips):
            gv_copy(t, k).wait_recv()
            total += gvr[t, k].astype(F32)
        v_out[...] = v_prev[...] - rate_v * total
        if t + 1 < ITERS:
            vbuf[t + 1, me_p] = v_out[...].astype(BF)
            date_start(t + 1)

    u_prev, v_prev = u_ref, v_ref
    if square:
        u_square(0, 0).start()
        u_square(0, 1).start()
    date_start(0)
    if square:
        u_square(0, 2).start()
        u_square(0, 3).start()
    for t in range(ITERS):
        if not square:
            for s in range(1, n_date):
                u_copy(t, s).start()
        elif t == 0:
            pixel_pass(t)
        date_pass(t)
        if square and t > 0:
            pixel_pass(t)
        date_panel(t)
        if t == 0:
            load_o.wait()
        gvt[...] = jnp.zeros_like(gvt)

        if square:
            for i, source, h in (
                (None, me_d, 0), (None, me_d, 1), (0, xn, 0), (1, yn, 1),
                (2, xn, 1), (3, yn, 0), (4, diag, 0), (5, diag, 1),
            ):
                if i is not None:
                    if i > 1:
                        u_square(t, i).wait_recv()
                gu, gv = tile(t, source, h * half)
                gvt[...] += gv
                if i is None:
                    own_gu[h * half:(h + 1) * half, :] = gu
                elif i in (2, 3):
                    keep[i - 2] = gu
                else:
                    j = i if i < 2 else i - 2
                    gus[t, j] = gu.astype(BF)
                    gu_square(t, j).start()
        else:
            gu, gv = tile(t, me_d, 0)
            own_gu[...] = gu
            gvt[...] += gv

            def step(s, carry):
                u_copy(t, n_date - s).wait_recv()
                gu, gv = tile(t, at_date(s), 0)
                gus[t, s] = gu.astype(BF)
                gvt[...] += gv
                gu_copy(t, s).start()
                return carry

            lax.fori_loop(1, n_date, step, 0)

        date_grad_send(t)
        date_grad_pass(t)
        if square:
            for i, kept in ((4, 1), (5, 0)):
                gu_square(t, i - 2).wait_recv()
                gus[t, i] = (keep[kept] + gur[t, i - 2].astype(F32)).astype(BF)
                gu_square(t, i).start()
        date_update(t, v_prev)
        if square:
            for h in range(2):
                rows = slice(h * half, (h + 1) * half)
                gu_square(t, h).wait_recv()
                gu_square(t, 4 + h).wait_recv()
                total = own_gu[rows, :] + gur[t, h].astype(F32) + gur[t, 4 + h].astype(F32)
                u_out[rows, :] = u_prev[rows, :] - rate_u * total
                if t + 1 < ITERS:
                    ubuf[t + 1, me_d, rows, :] = u_out[rows, :].astype(BF)
                    for i in ((0, 3), (1, 2))[h]:
                        u_square(t + 1, i).start()
        else:
            total = own_gu[...]
            for s in range(1, n_date):
                gu_copy(t, s).wait_recv()
                total += gur[t, s].astype(F32)
            u_out[...] = u_prev[...] - rate_u * total
            if t + 1 < ITERS:
                ubuf[t + 1, me_d] = u_out[...].astype(BF)
        u_prev, v_prev = u_out, v_out

    for t in range(ITERS):
        ge_copy(t).wait_send()
        for k in range(chips):
            v_pass(t, k).wait_send()
        for k in range(1, chips):
            v_copy(t, k).wait_send()
            gv_copy(t, k).wait_send()
        if square:
            for i in range(6):
                u_square(t, i).wait_send()
                gu_square(t, i).wait_send()
        else:
            for s in range(1, n_date):
                u_copy(t, s).wait_send()
                gu_copy(t, s).wait_send()


def shards(n_pix, n_date, pixel_factor, date_factor, clear_obs, clear_blocks, clear_count):
    ru, rank = pixel_factor.shape
    rv = date_factor.shape[0]
    devices = n_pix * n_date
    cap = clear_obs.shape[2]
    cols = n_pix * rv
    blocks_in_tile = (n_date * ru // BLOCK) * (cols // BLOCK)
    match = (clear_blocks[0, 0][None, :] == jnp.arange(blocks_in_tile)[:, None]) & (
        jnp.arange(cap)[None, :] < clear_count[0, 0]
    )
    slot = jnp.sum(jnp.where(match, jnp.arange(cap)[None, :], 0), axis=1).astype(jnp.int32)
    live = jnp.sum(match.astype(F32), axis=1)
    body = functools.partial(
        kernel, n_pix, n_date, 64.0 / (rv * devices), 64.0 / (ru * devices)
    )
    chips = n_pix // 2
    square = n_date == 4 and ru % (2 * BLOCK) == 0
    piece = ru // 2 if square else ru
    parts = 6 if square else n_date
    vmem = pl.BlockSpec(memory_space=pltpu.VMEM)
    smem = pl.BlockSpec(memory_space=pltpu.SMEM)
    hbm = pl.BlockSpec(memory_space=pl.ANY)
    dma = pltpu.SemaphoreType.DMA
    return pl.pallas_call(
        body,
        out_shape=(
            jax.ShapeDtypeStruct((ru, rank), F32),
            jax.ShapeDtypeStruct((rv, rank), F32),
        ),
        in_specs=[smem, smem, hbm, hbm, hbm],
        out_specs=(vmem, vmem),
        scratch_shapes=[
            pltpu.VMEM((ru, rank), F32),
            pltpu.VMEM((rv, rank), F32),
            pltpu.VMEM((cap, BLOCK, BLOCK), BF),
            pltpu.VMEM((ITERS, n_date, ru, rank), BF),
            pltpu.VMEM((ITERS, n_pix, rv, rank), BF),
            pltpu.VMEM((ITERS, parts, piece, rank), BF),
            pltpu.VMEM((ITERS, parts, piece, rank), BF),
            pltpu.VMEM((n_pix, rv, rank), F32),
            pltpu.VMEM((ITERS, chips, rv, rank), BF),
            pltpu.VMEM((ITERS, chips, rv, rank), BF),
            pltpu.VMEM((ITERS, chips, rv, rank), BF),
            pltpu.VMEM((ITERS, chips, rv, rank), BF),
            pltpu.VMEM((cols, rank), BF),
            pltpu.VMEM((piece, cols), BF),
            pltpu.VMEM((rank, cols), F32),
            pltpu.VMEM((ru, rank), F32),
            pltpu.VMEM((2, piece, rank), F32),
            dma((3,)),
            dma((ITERS, parts)), dma((ITERS, parts)),
            dma((ITERS, chips)), dma((ITERS, chips)),
            dma((ITERS, chips)), dma((ITERS, chips)),
            dma((ITERS, parts)), dma((ITERS, parts)),
            dma((ITERS, chips)), dma((ITERS, chips)),
            dma((ITERS,)), dma((ITERS,)),
        ],
        compiler_params=pltpu.CompilerParams(
            collective_id=0, has_side_effects=True, vmem_limit_bytes=60 * 1024 * 1024
        ),
    )(slot, live, pixel_factor, date_factor, clear_obs.reshape(cap, BLOCK, BLOCK))


def solution(mesh):
    in_specs = (
        P(("pix", "date"), None),
        P(("date", "pix"), None),
        P("pix", "date", None, None, None),
        P("pix", "date", None),
        P("pix", "date"),
    )
    out_specs = (P(("pix", "date"), None), P(("date", "pix"), None))
    body = functools.partial(shards, mesh.shape["pix"], mesh.shape["date"])
    return jax.shard_map(body, mesh=mesh, in_specs=in_specs, out_specs=out_specs, check_vma=False)
```

```python
import functools

import jax
import jax.numpy as jnp
from jax import lax
from jax.experimental import pallas as pl
from jax.experimental.pallas import tpu as pltpu
from jax.sharding import PartitionSpec as P

BLOCK = 128
ITERS = 2
MESH = pl.DeviceIdType.MESH
BF = jnp.bfloat16
F32 = jnp.float32


def dot(a, b, ca, cb):
    return lax.dot_general(a, b, (((ca,), (cb,)), ((), ())), preferred_element_type=F32)


def kernel(
    n_pix, n_date, rate_u, rate_v,
    table_ref, u_hbm, v_hbm, obs_hbm, u_out, v_out,
    u_ref, v_ref, obs, ubuf, vbuf, gus, gur, gvf, gvs, gvr, gve, gvo, vpan, vpant, mbuf, gvt, own_gu, keep,
    load_sem, us, ur, vs, vr, ws, wr, gu_s, gu_r, gv_s, gv_r, ge_s, ge_r,
):
    me_p = lax.axis_index("pix")
    me_d = lax.axis_index("date")
    ru, rank = u_ref.shape
    rv = v_ref.shape[0]
    cols = n_pix * rv
    cb = cols // BLOCK
    chips = n_pix // 2
    square = n_date == 4 and ru % (2 * BLOCK) == 0
    half = ru // 2
    piece = mbuf.shape[0]
    nb = piece // BLOCK

    load_u = pltpu.make_async_copy(u_hbm, u_ref, load_sem.at[0])
    load_v = pltpu.make_async_copy(v_hbm, v_ref, load_sem.at[1])
    load_o = pltpu.make_async_copy(obs_hbm, obs, load_sem.at[2])
    load_u.start()
    load_v.start()
    load_o.start()

    core = lax.rem(me_p, 2)
    sib = me_p + 1 - 2 * core

    def at_date(s):
        return lax.rem(me_d + s, n_date)

    def at_chip(k):
        return lax.rem(me_p + 2 * k, n_pix)

    xn = me_d + 1 - 2 * lax.rem(me_d, 2)
    yn = lax.rem(me_d + 2, n_date)
    diag = lax.rem(xn + 2, n_date)

    def copy(src, dst, ssem, rsem, p, d):
        return pltpu.make_async_remote_copy(
            src_ref=src, dst_ref=dst, send_sem=ssem, recv_sem=rsem, device_id=(p, d), device_id_type=MESH
        )

    def v_copy(t, k):
        return copy(vbuf.at[t, me_p], vbuf.at[t, me_p], vs.at[t, k], vr.at[t, k], at_chip(k), me_d)

    def v_pass(t, k):
        held = vbuf.at[t, at_chip(chips - k)]
        return copy(held, held, ws.at[t, k], wr.at[t, k], sib, me_d)

    def ge_copy(t):
        return copy(gve.at[t], gvo.at[t], ge_s.at[t], ge_r.at[t], sib, me_d)

    def gv_copy(t, k):
        return copy(gvs.at[t, k], gvr.at[t, k], gv_s.at[t, k], gv_r.at[t, k], at_chip(k), me_d)

    def u_copy(t, s):
        return copy(ubuf.at[t, me_d], ubuf.at[t, me_d], us.at[t, s], ur.at[t, s], me_p, at_date(s))

    def gu_copy(t, s):
        return copy(gus.at[t, s], gur.at[t, s], gu_s.at[t, s], gu_r.at[t, s], me_p, at_date(s))

    def u_square(t, i):
        owner, h, to = (
            (me_d, 0, xn), (me_d, 1, yn), (me_d, 1, xn), (me_d, 0, yn), (xn, 0, yn), (yn, 1, xn),
        )[i]
        part = ubuf.at[t, owner, pl.ds(h * half, half)]
        return copy(part, part, us.at[t, i], ur.at[t, i], me_p, to)

    def gu_square(t, i):
        to = xn if i in (0, 2, 5) else yn
        return copy(gus.at[t, i], gur.at[t, i], gu_s.at[t, i], gu_r.at[t, i], me_p, to)

    barrier = pltpu.get_barrier_semaphore()

    def greet(p, d):
        pl.semaphore_signal(barrier, inc=1, device_id=(p, d), device_id_type=MESH)

    greet(sib, me_d)
    for k in range(1, chips):
        greet(at_chip(k), me_d)
    if square:
        greet(me_p, xn)
        greet(me_p, yn)
    else:
        for s in range(1, n_date):
            greet(me_p, at_date(s))
    load_u.wait()
    ubuf[0, me_d] = u_ref[...].astype(BF)
    load_v.wait()
    vbuf[0, me_p] = v_ref[...].astype(BF)
    pl.semaphore_wait(barrier, chips + (2 if square else n_date - 1))

    def tile(t, source, start):
        uc = ubuf.at[t, source, pl.ds(start, piece)]
        base = source * (ru // BLOCK) + start // BLOCK

        predicted = dot(uc[...], vpant[...], 1, 0)
        for ib in range(nb):
            for j in range(cb):
                code = table_ref[(base + ib) * cb + j]
                o = obs[jnp.maximum(code, 0)].astype(F32)
                here = (slice(ib * BLOCK, (ib + 1) * BLOCK), slice(j * BLOCK, (j + 1) * BLOCK))
                m = (predicted[here] - o) * jnp.where(code >= 0, 1.0, 0.0)
                mbuf[here] = m.astype(BF)
        misfit = mbuf[...]
        return dot(misfit, vpan[...], 1, 0), dot(uc[...], misfit, 0, 0)

    def date_start(t):
        for k in range(1, chips):
            v_copy(t, k).start()
        v_pass(t, 0).start()

    def date_pass(t):
        for k in range(1, chips):
            v_copy(t, k).wait_recv()
            v_pass(t, k).start()

    def date_panel(t):
        for k in range(chips):
            v_pass(t, k).wait_recv()
        panel = vbuf[t]
        if rv % 16:
            panel = panel.astype(F32)
        vpan[...] = panel.reshape(cols, rank).astype(BF)
        vpant[...] = vpan[...].T

    def pixel_pass(t):
        u_square(t, 0).wait_recv()
        u_square(t, 4).start()
        u_square(t, 1).wait_recv()
        u_square(t, 5).start()

    def date_grad_send(t):
        gvf[...] = gvt[...].T.reshape(n_pix, rv, rank)
        for k in range(chips):
            gve[t, k] = gvf[2 * k + 1 - core].astype(BF)
        ge_copy(t).start()

    def date_grad_pass(t):
        ge_copy(t).wait_recv()
        chip = me_p // 2
        for k in range(1, chips):
            to = lax.rem(chip + k, chips)
            gvs[t, k] = (gvf[2 * to + core] + gvo[t, to].astype(F32)).astype(BF)
            gv_copy(t, k).start()

    def date_update(t, v_prev):
        total = gvf[me_p] + gvo[t, me_p // 2].astype(F32)
        for k in range(1, chips):
            gv_copy(t, k).wait_recv()
            total += gvr[t, k].astype(F32)
        v_out[...] = v_prev[...] - rate_v * total
        if t + 1 < ITERS:
            vbuf[t + 1, me_p] = v_out[...].astype(BF)
            date_start(t + 1)

    u_prev, v_prev = u_ref, v_ref
    if square:
        u_square(0, 0).start()
        u_square(0, 1).start()
    date_start(0)
    if square:
        u_square(0, 2).start()
        u_square(0, 3).start()
    for t in range(ITERS):
        if not square:
            for s in range(1, n_date):
                u_copy(t, s).start()
        elif t == 0:
            pixel_pass(t)
        date_pass(t)
        if square and t > 0:
            pixel_pass(t)
        date_panel(t)
        if t == 0:
            load_o.wait()
        gvt[...] = jnp.zeros_like(gvt)

        if square:
            for i, source, h in (
                (0, xn, 0), (1, yn, 1), (4, diag, 0), (5, diag, 1),
                (2, xn, 1), (3, yn, 0), (None, me_d, 0), (None, me_d, 1),
            ):
                if i is not None:
                    if i > 1:
                        u_square(t, i).wait_recv()
                gu, gv = tile(t, source, h * half)
                gvt[...] += gv
                if i is None:
                    own_gu[h * half:(h + 1) * half, :] = gu
                    gu_square(t, 2 + h).wait_recv()
                    gus[t, 4 + h] = (keep[1 - h] + gur[t, 2 + h].astype(F32)).astype(BF)
                    gu_square(t, 4 + h).start()
                elif i in (2, 3):
                    keep[i - 2] = gu
                else:
                    j = i if i < 2 else i - 2
                    gus[t, j] = gu.astype(BF)
                    gu_square(t, j).start()
        else:
            gu, gv = tile(t, me_d, 0)
            own_gu[...] = gu
            gvt[...] += gv

            def step(s, carry):
                u_copy(t, n_date - s).wait_recv()
                gu, gv = tile(t, at_date(s), 0)
                gus[t, s] = gu.astype(BF)
                gvt[...] += gv
                gu_copy(t, s).start()
                return carry

            lax.fori_loop(1, n_date, step, 0)

        date_grad_send(t)
        date_grad_pass(t)
        date_update(t, v_prev)
        if square:
            for h in range(2):
                rows = slice(h * half, (h + 1) * half)
                gu_square(t, h).wait_recv()
                gu_square(t, 4 + h).wait_recv()
                total = own_gu[rows, :] + gur[t, h].astype(F32) + gur[t, 4 + h].astype(F32)
                u_out[rows, :] = u_prev[rows, :] - rate_u * total
                if t + 1 < ITERS:
                    ubuf[t + 1, me_d, rows, :] = u_out[rows, :].astype(BF)
                    for i in ((0, 3), (1, 2))[h]:
                        u_square(t + 1, i).start()
        else:
            total = own_gu[...]
            for s in range(1, n_date):
                gu_copy(t, s).wait_recv()
                total += gur[t, s].astype(F32)
            u_out[...] = u_prev[...] - rate_u * total
            if t + 1 < ITERS:
                ubuf[t + 1, me_d] = u_out[...].astype(BF)
        u_prev, v_prev = u_out, v_out

    for t in range(ITERS):
        ge_copy(t).wait_send()
        for k in range(chips):
            v_pass(t, k).wait_send()
        for k in range(1, chips):
            v_copy(t, k).wait_send()
            gv_copy(t, k).wait_send()
        if square:
            for i in range(6):
                u_square(t, i).wait_send()
                gu_square(t, i).wait_send()
        else:
            for s in range(1, n_date):
                u_copy(t, s).wait_send()
                gu_copy(t, s).wait_send()


def shards(n_pix, n_date, pixel_factor, date_factor, clear_obs, clear_blocks, clear_count):
    ru, rank = pixel_factor.shape
    rv = date_factor.shape[0]
    devices = n_pix * n_date
    cap = clear_obs.shape[2]
    cols = n_pix * rv
    blocks_in_tile = (n_date * ru // BLOCK) * (cols // BLOCK)
    match = (clear_blocks[0, 0][None, :] == jnp.arange(blocks_in_tile)[:, None]) & (
        jnp.arange(cap)[None, :] < clear_count[0, 0]
    )
    table = jnp.max(jnp.where(match, jnp.arange(cap)[None, :], -1), axis=1).astype(jnp.int32)
    body = functools.partial(
        kernel, n_pix, n_date, 64.0 / (rv * devices), 64.0 / (ru * devices)
    )
    chips = n_pix // 2
    square = n_date == 4 and ru % (2 * BLOCK) == 0
    piece = ru // 2 if square else ru
    parts = 6 if square else n_date
    vmem = pl.BlockSpec(memory_space=pltpu.VMEM)
    smem = pl.BlockSpec(memory_space=pltpu.SMEM)
    hbm = pl.BlockSpec(memory_space=pl.ANY)
    dma = pltpu.SemaphoreType.DMA
    return pl.pallas_call(
        body,
        out_shape=(
            jax.ShapeDtypeStruct((ru, rank), F32),
            jax.ShapeDtypeStruct((rv, rank), F32),
        ),
        in_specs=[smem, hbm, hbm, hbm],
        out_specs=(vmem, vmem),
        scratch_shapes=[
            pltpu.VMEM((ru, rank), F32),
            pltpu.VMEM((rv, rank), F32),
            pltpu.VMEM((cap, BLOCK, BLOCK), BF),
            pltpu.VMEM((ITERS, n_date, ru, rank), BF),
            pltpu.VMEM((ITERS, n_pix, rv, rank), BF),
            pltpu.VMEM((ITERS, parts, piece, rank), BF),
            pltpu.VMEM((ITERS, parts, piece, rank), BF),
            pltpu.VMEM((n_pix, rv, rank), F32),
            pltpu.VMEM((ITERS, chips, rv, rank), BF),
            pltpu.VMEM((ITERS, chips, rv, rank), BF),
            pltpu.VMEM((ITERS, chips, rv, rank), BF),
            pltpu.VMEM((ITERS, chips, rv, rank), BF),
            pltpu.VMEM((cols, rank), BF),
            pltpu.VMEM((rank, cols), BF),
            pltpu.VMEM((piece, cols), BF),
            pltpu.VMEM((rank, cols), F32),
            pltpu.VMEM((ru, rank), F32),
            pltpu.VMEM((2, piece, rank), F32),
            dma((3,)),
            dma((ITERS, parts)), dma((ITERS, parts)),
            dma((ITERS, chips)), dma((ITERS, chips)),
            dma((ITERS, chips)), dma((ITERS, chips)),
            dma((ITERS, parts)), dma((ITERS, parts)),
            dma((ITERS, chips)), dma((ITERS, chips)),
            dma((ITERS,)), dma((ITERS,)),
        ],
        compiler_params=pltpu.CompilerParams(
            collective_id=0, has_side_effects=True, vmem_limit_bytes=60 * 1024 * 1024
        ),
    )(table, pixel_factor, date_factor, clear_obs.reshape(cap, BLOCK, BLOCK))


def solution(mesh):
    in_specs = (
        P(("pix", "date"), None),
        P(("date", "pix"), None),
        P("pix", "date", None, None, None),
        P("pix", "date", None),
        P("pix", "date"),
    )
    out_specs = (P(("pix", "date"), None), P(("date", "pix"), None))
    body = functools.partial(shards, mesh.shape["pix"], mesh.shape["date"])
    return jax.shard_map(body, mesh=mesh, in_specs=in_specs, out_specs=out_specs, check_vma=False)
```

```python
import functools

import jax
import jax.numpy as jnp
from jax import lax
from jax.experimental import pallas as pl
from jax.experimental.pallas import tpu as pltpu
from jax.sharding import PartitionSpec as P

BLOCK = 128
ITERS = 2
MESH = pl.DeviceIdType.MESH
BF = jnp.bfloat16
F32 = jnp.float32


def dot(a, b, ca, cb):
    return lax.dot_general(a, b, (((ca,), (cb,)), ((), ())), preferred_element_type=F32)


def kernel(
    n_pix, n_date, rate_u, rate_v,
    table_ref, u_hbm, v_hbm, obs_hbm, u_out, v_out,
    u_ref, v_ref, obs, ubuf, vbuf, gus, gur, gvf, gvs, gvr, gve, gvo, vpan, vpant, mbuf, gvt, own_gu, keep,
    load_sem, us, ur, vs, vr, ws, wr, gu_s, gu_r, gv_s, gv_r, ge_s, ge_r,
):
    me_p = lax.axis_index("pix")
    me_d = lax.axis_index("date")
    ru, rank = u_ref.shape
    rv = v_ref.shape[0]
    cols = n_pix * rv
    cb = cols // BLOCK
    chips = n_pix // 2
    square = n_date == 4 and ru % (2 * BLOCK) == 0
    half = ru // 2
    piece = mbuf.shape[0]
    nb = piece // BLOCK

    load_u = pltpu.make_async_copy(u_hbm, u_ref, load_sem.at[0])
    load_v = pltpu.make_async_copy(v_hbm, v_ref, load_sem.at[1])
    load_o = pltpu.make_async_copy(obs_hbm, obs, load_sem.at[2])
    load_u.start()
    load_v.start()
    load_o.start()

    core = lax.rem(me_p, 2)
    sib = me_p + 1 - 2 * core

    def at_date(s):
        return lax.rem(me_d + s, n_date)

    def at_chip(k):
        return lax.rem(me_p + 2 * k, n_pix)

    xn = me_d + 1 - 2 * lax.rem(me_d, 2)
    yn = lax.rem(me_d + 2, n_date)
    diag = lax.rem(xn + 2, n_date)

    def copy(src, dst, ssem, rsem, p, d):
        return pltpu.make_async_remote_copy(
            src_ref=src, dst_ref=dst, send_sem=ssem, recv_sem=rsem, device_id=(p, d), device_id_type=MESH
        )

    def v_copy(t, k):
        return copy(vbuf.at[t, me_p], vbuf.at[t, me_p], vs.at[t, k], vr.at[t, k], at_chip(k), me_d)

    def v_pass(t, k):
        held = vbuf.at[t, at_chip(chips - k)]
        return copy(held, held, ws.at[t, k], wr.at[t, k], sib, me_d)

    def ge_copy(t):
        return copy(gve.at[t], gvo.at[t], ge_s.at[t], ge_r.at[t], sib, me_d)

    def gv_copy(t, k):
        return copy(gvs.at[t, k], gvr.at[t, k], gv_s.at[t, k], gv_r.at[t, k], at_chip(k), me_d)

    def u_copy(t, s):
        return copy(ubuf.at[t, me_d], ubuf.at[t, me_d], us.at[t, s], ur.at[t, s], me_p, at_date(s))

    def gu_copy(t, s):
        return copy(gus.at[t, s], gur.at[t, s], gu_s.at[t, s], gu_r.at[t, s], me_p, at_date(s))

    def u_square(t, i):
        owner, h, to = (
            (me_d, 0, xn), (me_d, 1, yn), (me_d, 1, xn), (me_d, 0, yn), (xn, 0, yn), (yn, 1, xn),
        )[i]
        part = ubuf.at[t, owner, pl.ds(h * half, half)]
        return copy(part, part, us.at[t, i], ur.at[t, i], me_p, to)

    def gu_square(t, i):
        to = xn if i in (0, 2, 5) else yn
        return copy(gus.at[t, i], gur.at[t, i], gu_s.at[t, i], gu_r.at[t, i], me_p, to)

    barrier = pltpu.get_barrier_semaphore()

    def greet(p, d):
        pl.semaphore_signal(barrier, inc=1, device_id=(p, d), device_id_type=MESH)

    greet(sib, me_d)
    for k in range(1, chips):
        greet(at_chip(k), me_d)
    if square:
        greet(me_p, xn)
        greet(me_p, yn)
    else:
        for s in range(1, n_date):
            greet(me_p, at_date(s))
    load_u.wait()
    ubuf[0, me_d] = u_ref[...].astype(BF)
    load_v.wait()
    vbuf[0, me_p] = v_ref[...].astype(BF)
    pl.semaphore_wait(barrier, chips + (2 if square else n_date - 1))

    def tile(t, source, start):
        uc = ubuf.at[t, source, pl.ds(start, piece)]
        base = source * (ru // BLOCK) + start // BLOCK

        predicted = dot(uc[...], vpant[...], 1, 0)
        for ib in range(nb):
            for j in range(cb):
                code = table_ref[(base + ib) * cb + j]
                o = obs[jnp.maximum(code, 0)].astype(F32)
                here = (slice(ib * BLOCK, (ib + 1) * BLOCK), slice(j * BLOCK, (j + 1) * BLOCK))
                m = (predicted[here] - o) * jnp.where(code >= 0, 1.0, 0.0)
                mbuf[here] = m.astype(BF)
        misfit = mbuf[...]
        return dot(misfit, vpan[...], 1, 0), dot(uc[...], misfit, 0, 0)

    def date_start(t):
        for k in range(1, chips):
            v_copy(t, k).start()
        v_pass(t, 0).start()

    def date_pass(t):
        for k in range(1, chips):
            v_copy(t, k).wait_recv()
            v_pass(t, k).start()

    def date_panel(t):
        for k in range(chips):
            v_pass(t, k).wait_recv()
        panel = vbuf[t]
        if rv % 16:
            panel = panel.astype(F32)
        vpan[...] = panel.reshape(cols, rank).astype(BF)
        vpant[...] = vpan[...].T

    def pixel_pass(t):
        u_square(t, 0).wait_recv()
        u_square(t, 4).start()
        u_square(t, 1).wait_recv()
        u_square(t, 5).start()

    def date_grad_send(t):
        gvf[...] = gvt[...].T.reshape(n_pix, rv, rank)
        for k in range(chips):
            gve[t, k] = gvf[2 * k + 1 - core].astype(BF)
        ge_copy(t).start()

    def date_grad_pass(t):
        ge_copy(t).wait_recv()
        chip = me_p // 2
        for k in range(1, chips):
            to = lax.rem(chip + k, chips)
            gvs[t, k] = (gvf[2 * to + core] + gvo[t, to].astype(F32)).astype(BF)
            gv_copy(t, k).start()

    def date_update(t, v_prev):
        total = gvf[me_p] + gvo[t, me_p // 2].astype(F32)
        for k in range(1, chips):
            gv_copy(t, k).wait_recv()
            total += gvr[t, k].astype(F32)
        v_out[...] = v_prev[...] - rate_v * total
        if t + 1 < ITERS:
            vbuf[t + 1, me_p] = v_out[...].astype(BF)
            date_start(t + 1)

    u_prev, v_prev = u_ref, v_ref
    if square:
        u_square(0, 0).start()
        u_square(0, 1).start()
    date_start(0)
    if square:
        u_square(0, 2).start()
        u_square(0, 3).start()
    for t in range(ITERS):
        if not square:
            for s in range(1, n_date):
                u_copy(t, s).start()
        else:
            pixel_pass(t)
        date_pass(t)
        date_panel(t)
        if t == 0:
            load_o.wait()
        gvt[...] = jnp.zeros_like(gvt)

        if square:
            for i, source, h in (
                (0, xn, 0), (1, yn, 1), (4, diag, 0), (5, diag, 1),
                (2, xn, 1), (3, yn, 0), (None, me_d, 0), (None, me_d, 1),
            ):
                if i is not None:
                    if i > 1:
                        u_square(t, i).wait_recv()
                gu, gv = tile(t, source, h * half)
                gvt[...] += gv
                if i is None:
                    own_gu[h * half:(h + 1) * half, :] = gu
                    gu_square(t, 2 + h).wait_recv()
                    gus[t, 4 + h] = (keep[1 - h] + gur[t, 2 + h].astype(F32)).astype(BF)
                    gu_square(t, 4 + h).start()
                elif i in (2, 3):
                    keep[i - 2] = gu
                else:
                    j = i if i < 2 else i - 2
                    gus[t, j] = gu.astype(BF)
                    gu_square(t, j).start()
        else:
            gu, gv = tile(t, me_d, 0)
            own_gu[...] = gu
            gvt[...] += gv

            def step(s, carry):
                u_copy(t, n_date - s).wait_recv()
                gu, gv = tile(t, at_date(s), 0)
                gus[t, s] = gu.astype(BF)
                gvt[...] += gv
                gu_copy(t, s).start()
                return carry

            lax.fori_loop(1, n_date, step, 0)

        date_grad_send(t)
        date_grad_pass(t)
        if square:
            for h in range(2):
                rows = slice(h * half, (h + 1) * half)
                gu_square(t, h).wait_recv()
                gu_square(t, 4 + h).wait_recv()
                total = own_gu[rows, :] + gur[t, h].astype(F32) + gur[t, 4 + h].astype(F32)
                u_out[rows, :] = u_prev[rows, :] - rate_u * total
                if t + 1 < ITERS:
                    ubuf[t + 1, me_d, rows, :] = u_out[rows, :].astype(BF)
                    for i in ((0, 3), (1, 2))[h]:
                        u_square(t + 1, i).start()
        else:
            total = own_gu[...]
            for s in range(1, n_date):
                gu_copy(t, s).wait_recv()
                total += gur[t, s].astype(F32)
            u_out[...] = u_prev[...] - rate_u * total
            if t + 1 < ITERS:
                ubuf[t + 1, me_d] = u_out[...].astype(BF)
        date_update(t, v_prev)
        u_prev, v_prev = u_out, v_out

    for t in range(ITERS):
        ge_copy(t).wait_send()
        for k in range(chips):
            v_pass(t, k).wait_send()
        for k in range(1, chips):
            v_copy(t, k).wait_send()
            gv_copy(t, k).wait_send()
        if square:
            for i in range(6):
                u_square(t, i).wait_send()
                gu_square(t, i).wait_send()
        else:
            for s in range(1, n_date):
                u_copy(t, s).wait_send()
                gu_copy(t, s).wait_send()


def shards(n_pix, n_date, pixel_factor, date_factor, clear_obs, clear_blocks, clear_count):
    ru, rank = pixel_factor.shape
    rv = date_factor.shape[0]
    devices = n_pix * n_date
    cap = clear_obs.shape[2]
    cols = n_pix * rv
    blocks_in_tile = (n_date * ru // BLOCK) * (cols // BLOCK)
    match = (clear_blocks[0, 0][None, :] == jnp.arange(blocks_in_tile)[:, None]) & (
        jnp.arange(cap)[None, :] < clear_count[0, 0]
    )
    table = jnp.max(jnp.where(match, jnp.arange(cap)[None, :], -1), axis=1).astype(jnp.int32)
    body = functools.partial(
        kernel, n_pix, n_date, 64.0 / (rv * devices), 64.0 / (ru * devices)
    )
    chips = n_pix // 2
    square = n_date == 4 and ru % (2 * BLOCK) == 0
    piece = ru // 2 if square else ru
    parts = 6 if square else n_date
    vmem = pl.BlockSpec(memory_space=pltpu.VMEM)
    smem = pl.BlockSpec(memory_space=pltpu.SMEM)
    hbm = pl.BlockSpec(memory_space=pl.ANY)
    dma = pltpu.SemaphoreType.DMA
    return pl.pallas_call(
        body,
        out_shape=(
            jax.ShapeDtypeStruct((ru, rank), F32),
            jax.ShapeDtypeStruct((rv, rank), F32),
        ),
        in_specs=[smem, hbm, hbm, hbm],
        out_specs=(vmem, vmem),
        scratch_shapes=[
            pltpu.VMEM((ru, rank), F32),
            pltpu.VMEM((rv, rank), F32),
            pltpu.VMEM((cap, BLOCK, BLOCK), BF),
            pltpu.VMEM((ITERS, n_date, ru, rank), BF),
            pltpu.VMEM((ITERS, n_pix, rv, rank), BF),
            pltpu.VMEM((ITERS, parts, piece, rank), BF),
            pltpu.VMEM((ITERS, parts, piece, rank), BF),
            pltpu.VMEM((n_pix, rv, rank), F32),
            pltpu.VMEM((ITERS, chips, rv, rank), BF),
            pltpu.VMEM((ITERS, chips, rv, rank), BF),
            pltpu.VMEM((ITERS, chips, rv, rank), BF),
            pltpu.VMEM((ITERS, chips, rv, rank), BF),
            pltpu.VMEM((cols, rank), BF),
            pltpu.VMEM((rank, cols), BF),
            pltpu.VMEM((piece, cols), BF),
            pltpu.VMEM((rank, cols), F32),
            pltpu.VMEM((ru, rank), F32),
            pltpu.VMEM((2, piece, rank), F32),
            dma((3,)),
            dma((ITERS, parts)), dma((ITERS, parts)),
            dma((ITERS, chips)), dma((ITERS, chips)),
            dma((ITERS, chips)), dma((ITERS, chips)),
            dma((ITERS, parts)), dma((ITERS, parts)),
            dma((ITERS, chips)), dma((ITERS, chips)),
            dma((ITERS,)), dma((ITERS,)),
        ],
        compiler_params=pltpu.CompilerParams(
            collective_id=0, has_side_effects=True, vmem_limit_bytes=60 * 1024 * 1024
        ),
    )(table, pixel_factor, date_factor, clear_obs.reshape(cap, BLOCK, BLOCK))


def solution(mesh):
    in_specs = (
        P(("pix", "date"), None),
        P(("date", "pix"), None),
        P("pix", "date", None, None, None),
        P("pix", "date", None),
        P("pix", "date"),
    )
    out_specs = (P(("pix", "date"), None), P(("date", "pix"), None))
    body = functools.partial(shards, mesh.shape["pix"], mesh.shape["date"])
    return jax.shard_map(body, mesh=mesh, in_specs=in_specs, out_specs=out_specs, check_vma=False)
```

```python
import functools

import jax
import jax.numpy as jnp
from jax import lax
from jax.experimental import pallas as pl
from jax.experimental.pallas import tpu as pltpu
from jax.sharding import PartitionSpec as P

BLOCK = 128
ITERS = 2
MESH = pl.DeviceIdType.MESH
BF = jnp.bfloat16
F32 = jnp.float32


def dot(a, b, ca, cb):
    return lax.dot_general(a, b, (((ca,), (cb,)), ((), ())), preferred_element_type=F32)


def kernel(
    n_pix, n_date, rate_u, rate_v,
    table_ref, u_hbm, v_hbm, obs_hbm, u_out, v_out,
    u_ref, v_ref, obs, ubuf, vbuf, gus, gur, gvf, gvs, gvr, gve, gvo, vpan, vpant, mbuf, gvt, own_gu, keep,
    load_sem, us, ur, vs, vr, ws, wr, gu_s, gu_r, gv_s, gv_r, ge_s, ge_r,
):
    me_p = lax.axis_index("pix")
    me_d = lax.axis_index("date")
    ru, rank = u_ref.shape
    rv = v_ref.shape[0]
    cols = n_pix * rv
    cb = cols // BLOCK
    chips = n_pix // 2
    square = n_date == 4 and ru % (2 * BLOCK) == 0
    half = ru // 2
    piece = mbuf.shape[0]
    nb = piece // BLOCK

    load_u = pltpu.make_async_copy(u_hbm, u_ref, load_sem.at[0])
    load_v = pltpu.make_async_copy(v_hbm, v_ref, load_sem.at[1])
    load_o = pltpu.make_async_copy(obs_hbm, obs, load_sem.at[2])
    load_u.start()
    load_v.start()
    load_o.start()

    core = lax.rem(me_p, 2)
    sib = me_p + 1 - 2 * core

    def at_date(s):
        return lax.rem(me_d + s, n_date)

    def at_chip(k):
        return lax.rem(me_p + 2 * k, n_pix)

    xn = me_d + 1 - 2 * lax.rem(me_d, 2)
    yn = lax.rem(me_d + 2, n_date)
    diag = lax.rem(xn + 2, n_date)

    def copy(src, dst, ssem, rsem, p, d):
        return pltpu.make_async_remote_copy(
            src_ref=src, dst_ref=dst, send_sem=ssem, recv_sem=rsem, device_id=(p, d), device_id_type=MESH
        )

    def v_copy(t, k):
        return copy(vbuf.at[t, me_p], vbuf.at[t, me_p], vs.at[t, k], vr.at[t, k], at_chip(k), me_d)

    def v_pass(t, k):
        held = vbuf.at[t, at_chip(chips - k)]
        return copy(held, held, ws.at[t, k], wr.at[t, k], sib, me_d)

    def ge_copy(t):
        return copy(gve.at[t], gvo.at[t], ge_s.at[t], ge_r.at[t], sib, me_d)

    def gv_copy(t, k):
        return copy(gvs.at[t, k], gvr.at[t, k], gv_s.at[t, k], gv_r.at[t, k], at_chip(k), me_d)

    def u_copy(t, s):
        return copy(ubuf.at[t, me_d], ubuf.at[t, me_d], us.at[t, s], ur.at[t, s], me_p, at_date(s))

    def gu_copy(t, s):
        return copy(gus.at[t, s], gur.at[t, s], gu_s.at[t, s], gu_r.at[t, s], me_p, at_date(s))

    def u_square(t, i):
        owner, h, to = (
            (me_d, 0, xn), (me_d, 1, yn), (me_d, 1, xn), (me_d, 0, yn), (xn, 0, yn), (yn, 1, xn),
        )[i]
        part = ubuf.at[t, owner, pl.ds(h * half, half)]
        return copy(part, part, us.at[t, i], ur.at[t, i], me_p, to)

    def gu_square(t, i):
        to = xn if i in (0, 2, 5) else yn
        return copy(gus.at[t, i], gur.at[t, i], gu_s.at[t, i], gu_r.at[t, i], me_p, to)

    barrier = pltpu.get_barrier_semaphore()

    def greet(p, d):
        pl.semaphore_signal(barrier, inc=1, device_id=(p, d), device_id_type=MESH)

    greet(sib, me_d)
    for k in range(1, chips):
        greet(at_chip(k), me_d)
    if square:
        greet(me_p, xn)
        greet(me_p, yn)
    else:
        for s in range(1, n_date):
            greet(me_p, at_date(s))
    load_u.wait()
    ubuf[0, me_d] = u_ref[...].astype(BF)
    load_v.wait()
    vbuf[0, me_p] = v_ref[...].astype(BF)
    pl.semaphore_wait(barrier, chips + (2 if square else n_date - 1))

    def tile(t, source, start):
        uc = ubuf.at[t, source, pl.ds(start, piece)]
        base = source * (ru // BLOCK) + start // BLOCK

        predicted = dot(uc[...], vpant[...], 1, 0)
        for ib in range(nb):
            for j in range(cb):
                code = table_ref[(base + ib) * cb + j]
                o = obs[jnp.maximum(code, 0)].astype(F32)
                here = (slice(ib * BLOCK, (ib + 1) * BLOCK), slice(j * BLOCK, (j + 1) * BLOCK))
                m = (predicted[here] - o) * jnp.where(code >= 0, 1.0, 0.0)
                mbuf[here] = m.astype(BF)
        misfit = mbuf[...]
        return dot(misfit, vpan[...], 1, 0), dot(uc[...], misfit, 0, 0)

    def date_start(t):
        for k in range(1, chips):
            v_copy(t, k).start()
        v_pass(t, 0).start()

    def date_pass(t):
        for k in range(1, chips):
            v_copy(t, k).wait_recv()
            v_pass(t, k).start()

    def date_panel(t):
        for k in range(chips):
            v_pass(t, k).wait_recv()
        panel = vbuf[t]
        if rv % 16:
            panel = panel.astype(F32)
        vpan[...] = panel.reshape(cols, rank).astype(BF)
        vpant[...] = vpan[...].T

    def pixel_pass(t):
        u_square(t, 0).wait_recv()
        u_square(t, 4).start()
        u_square(t, 1).wait_recv()
        u_square(t, 5).start()

    def date_grad_send(t):
        gvf[...] = gvt[...].T.reshape(n_pix, rv, rank)
        for k in range(chips):
            gve[t, k] = gvf[2 * k + 1 - core].astype(BF)
        ge_copy(t).start()

    def date_grad_pass(t):
        ge_copy(t).wait_recv()
        chip = me_p // 2
        for k in range(1, chips):
            to = lax.rem(chip + k, chips)
            gvs[t, k] = (gvf[2 * to + core] + gvo[t, to].astype(F32)).astype(BF)
            gv_copy(t, k).start()

    def date_update(t, v_prev):
        total = gvf[me_p] + gvo[t, me_p // 2].astype(F32)
        for k in range(1, chips):
            gv_copy(t, k).wait_recv()
            total += gvr[t, k].astype(F32)
        v_out[...] = v_prev[...] - rate_v * total
        if t + 1 < ITERS:
            vbuf[t + 1, me_p] = v_out[...].astype(BF)
            date_start(t + 1)

    u_prev, v_prev = u_ref, v_ref
    if square:
        u_square(0, 0).start()
        u_square(0, 1).start()
    date_start(0)
    if square:
        u_square(0, 2).start()
        u_square(0, 3).start()
    for t in range(ITERS):
        if not square:
            for s in range(1, n_date):
                u_copy(t, s).start()
        else:
            pixel_pass(t)
        date_pass(t)
        date_panel(t)
        if t == 0:
            load_o.wait()
        gvt[...] = jnp.zeros_like(gvt)

        if square:
            for i, source, h in (
                (0, xn, 0), (1, yn, 1), (4, diag, 0), (5, diag, 1),
                (2, xn, 1), (3, yn, 0), (None, me_d, 0), (None, me_d, 1),
            ):
                if i is not None:
                    if i > 1:
                        u_square(t, i).wait_recv()
                gu, gv = tile(t, source, h * half)
                gvt[...] += gv
                if i is None:
                    own_gu[h * half:(h + 1) * half, :] = gu
                    gu_square(t, 2 + h).wait_recv()
                    gus[t, 4 + h] = (keep[1 - h] + gur[t, 2 + h].astype(F32)).astype(BF)
                    gu_square(t, 4 + h).start()
                elif i in (2, 3):
                    keep[i - 2] = gu
                else:
                    j = i if i < 2 else i - 2
                    gus[t, j] = gu.astype(BF)
                    gu_square(t, j).start()
        else:
            gu, gv = tile(t, me_d, 0)
            own_gu[...] = gu
            gvt[...] += gv

            def step(s, carry):
                u_copy(t, n_date - s).wait_recv()
                gu, gv = tile(t, at_date(s), 0)
                gus[t, s] = gu.astype(BF)
                gvt[...] += gv
                gu_copy(t, s).start()
                return carry

            lax.fori_loop(1, n_date, step, 0)

        date_grad_send(t)
        date_grad_pass(t)
        if square:
            for h in range(2):
                rows = slice(h * half, (h + 1) * half)
                gu_square(t, h).wait_recv()
                gu_square(t, 4 + h).wait_recv()
                total = own_gu[rows, :] + gur[t, h].astype(F32) + gur[t, 4 + h].astype(F32)
                u_out[rows, :] = u_prev[rows, :] - rate_u * total
                if t + 1 < ITERS:
                    ubuf[t + 1, me_d, rows, :] = u_out[rows, :].astype(BF)
                    for i in ((0, 3), (1, 2))[h]:
                        u_square(t + 1, i).start()
        else:
            total = own_gu[...]
            for s in range(1, n_date):
                gu_copy(t, s).wait_recv()
                total += gur[t, s].astype(F32)
            u_out[...] = u_prev[...] - rate_u * total
            if t + 1 < ITERS:
                ubuf[t + 1, me_d] = u_out[...].astype(BF)
        date_update(t, v_prev)
        u_prev, v_prev = u_out, v_out

    for t in range(ITERS):
        ge_copy(t).wait_send()
        for k in range(chips):
            v_pass(t, k).wait_send()
        for k in range(1, chips):
            v_copy(t, k).wait_send()
            gv_copy(t, k).wait_send()
        if square:
            for i in range(6):
                u_square(t, i).wait_send()
                gu_square(t, i).wait_send()
        else:
            for s in range(1, n_date):
                u_copy(t, s).wait_send()
                gu_copy(t, s).wait_send()


def shards(n_pix, n_date, pixel_factor, date_factor, clear_obs, clear_blocks, clear_count):
    ru, rank = pixel_factor.shape
    rv = date_factor.shape[0]
    devices = n_pix * n_date
    cap = clear_obs.shape[2]
    cols = n_pix * rv
    blocks_in_tile = (n_date * ru // BLOCK) * (cols // BLOCK)
    match = (clear_blocks[0, 0][None, :] == jnp.arange(blocks_in_tile)[:, None]) & (
        jnp.arange(cap)[None, :] < clear_count[0, 0]
    )
    table = jnp.max(jnp.where(match, jnp.arange(cap)[None, :], -1), axis=1).astype(jnp.int32)
    body = functools.partial(
        kernel, n_pix, n_date, 64.0 / (rv * devices), 64.0 / (ru * devices)
    )
    chips = n_pix // 2
    square = n_date == 4 and ru % (2 * BLOCK) == 0
    piece = ru // 2 if square else ru
    parts = 6 if square else n_date
    vmem = pl.BlockSpec(memory_space=pltpu.VMEM)
    smem = pl.BlockSpec(memory_space=pltpu.SMEM)
    hbm = pl.BlockSpec(memory_space=pl.ANY)
    dma = pltpu.SemaphoreType.DMA
    return pl.pallas_call(
        body,
        out_shape=(
            jax.ShapeDtypeStruct((ru, rank), F32),
            jax.ShapeDtypeStruct((rv, rank), F32),
        ),
        in_specs=[smem, hbm, hbm, hbm],
        out_specs=(vmem, vmem),
        scratch_shapes=[
            pltpu.VMEM((ru, rank), F32),
            pltpu.VMEM((rv, rank), F32),
            pltpu.VMEM((cap, BLOCK, BLOCK), BF),
            pltpu.VMEM((ITERS, n_date, ru, rank), BF),
            pltpu.VMEM((ITERS, n_pix, rv, rank), BF),
            pltpu.VMEM((ITERS, parts, piece, rank), BF),
            pltpu.VMEM((ITERS, parts, piece, rank), BF),
            pltpu.VMEM((n_pix, rv, rank), F32),
            pltpu.VMEM((ITERS, chips, rv, rank), BF),
            pltpu.VMEM((ITERS, chips, rv, rank), BF),
            pltpu.VMEM((ITERS, chips, rv, rank), BF),
            pltpu.VMEM((ITERS, chips, rv, rank), BF),
            pltpu.VMEM((cols, rank), BF),
            pltpu.VMEM((rank, cols), BF),
            pltpu.VMEM((piece, cols), BF),
            pltpu.VMEM((rank, cols), F32),
            pltpu.VMEM((ru, rank), F32),
            pltpu.VMEM((2, piece, rank), F32),
            dma((3,)),
            dma((ITERS, parts)), dma((ITERS, parts)),
            dma((ITERS, chips)), dma((ITERS, chips)),
            dma((ITERS, chips)), dma((ITERS, chips)),
            dma((ITERS, parts)), dma((ITERS, parts)),
            dma((ITERS, chips)), dma((ITERS, chips)),
            dma((ITERS,)), dma((ITERS,)),
        ],
        compiler_params=pltpu.CompilerParams(
            collective_id=0, has_side_effects=True, vmem_limit_bytes=53 * 1024 * 1024
        ),
    )(table, pixel_factor, date_factor, clear_obs.reshape(cap, BLOCK, BLOCK))


def solution(mesh):
    in_specs = (
        P(("pix", "date"), None),
        P(("date", "pix"), None),
        P("pix", "date", None, None, None),
        P("pix", "date", None),
        P("pix", "date"),
    )
    out_specs = (P(("pix", "date"), None), P(("date", "pix"), None))
    body = functools.partial(shards, mesh.shape["pix"], mesh.shape["date"])
    return jax.shard_map(body, mesh=mesh, in_specs=in_specs, out_specs=out_specs, check_vma=False)
```
